128 devices in a mesh: row: 8 (over z, y_lo), col: 16 (over y_hi, x, core).
Axes of the slice: x: 4, y: 4 (y_hi: 2, y_lo: 2; y = y_hi * 2 + y_lo), z: 4, core: 2. Of those that a mesh axis runs over, the one named last changes fastest.
Arguments:
- fock: bfloat16 [4096, 65536], P('row', 'col'), may hold values from -6 to 6
- pattern: int32 [64, 1024], P('row', 'col'), may hold values 0 or 1
- coeffs: bfloat16 [65536, 4096], P('col', 'row'), may hold values from -0.0390625 to 0.0390625
- order: int32 [64], replicated, may hold values from 0 to 63, as said below
Outputs:
- band_step: float32 [2, 2048, 4096], P(None, 'row', 'col')
The draws below stay inside these ranges and needn't reach their ends.
Inputs may be any that keep to these rules, and one draw needn't show every extreme that they name: `order`: a permutation of the atom blocks; the block at position p, with s = p mod (8), lies in a row tile t (t = block div (4)) with t mod 8 = s div (1).
All inputs are finite; a program needn't handle non-finite values. No bound on the sum of `pattern` on one device may be relied on, other than what follows from the above.
Results may differ from the reference program's by a relative error of at most 0.0003.
Values may be sent and summed in bfloat16 or wider, within the bound.
No kernel may reach another device: no remote copies, remote signals or barrier semaphores. Data moves between devices by JAX's collectives and lax.ppermute only.
A program may use at most 128 MiB of HBM per device.

```python
import jax
import jax.numpy as jnp
from jax import lax

ORDER = 65536
SLAB = 4096
BLK = 64
NB = 256
GRID_ROWS = 8


def draw_order(key, part):
    key = jax.random.fold_in(key, 7)
    slot_count = SLAB // (BLK * GRID_ROWS)
    per_pair = slot_count // GRID_ROWS
    tile_blocks = NB // BLK
    owner_keys = jax.random.split(key, GRID_ROWS)

    def shuffle_one(owner_key):
        return jax.random.permutation(owner_key, slot_count).astype(jnp.int32)
    shuffles = jax.vmap(shuffle_one)(owner_keys)
    picks = shuffles.reshape(GRID_ROWS, GRID_ROWS, per_pair).transpose(1, 0, 2)
    owners = jnp.arange(GRID_ROWS, dtype=jnp.int32)[None, :, None]
    atoms = (picks // tile_blocks * GRID_ROWS + owners) * tile_blocks + picks % tile_blocks
    return atoms.reshape(SLAB // BLK).astype(jnp.int32)


def plant(entries, rng, low, top_value):
    longest = entries.shape.index(max(entries.shape))
    spots = []
    for shift in (0, 1):
        where = [jax.random.randint(jax.random.fold_in(rng, axis), (), 0, length) for axis, length in enumerate(entries.shape)]
        where[longest] = (where[longest] + shift) % entries.shape[longest]
        spots.append(tuple(where))
    return entries.at[spots[0]].set(low).at[spots[1]].set(top_value)


def level_of(stream_key, shape, cuts, smallest, high):
    loudness = 1.0
    for axis_at, shards_of in cuts:
        draws = jax.random.uniform(jax.random.fold_in(jax.random.fold_in(stream_key, 6), axis_at), (shards_of,), jnp.float32, smallest / len(cuts), high / len(cuts))
        loudness = loudness * jnp.repeat(jnp.exp(draws), shape[axis_at] // shards_of).reshape((-1,) + (1,) * (len(shape) - 1 - axis_at))
    return loudness


def noise(rng, extent, deviation, bound, pieces=(), kind=jnp.bfloat16):
    level = level_of(rng, extent, pieces, -0.22, 0.18) if pieces else 1.0
    entries = jax.random.normal(rng, extent, jnp.float32) * deviation * level
    return jnp.minimum(jnp.maximum(entries, -bound), bound).astype(kind)


def setup_inputs(seed: int = 0) -> dict:
    key_list = jax.random.split(jax.random.key(seed), 5)
    return {
        "fock": noise(key_list[0], (SLAB, ORDER), 1.0, 6.0, ((0, 8), (1, 16))),
        "pattern": plant((jax.random.randint(key_list[1], (SLAB // BLK, ORDER // BLK), 0, 5) < 2).astype(jnp.int32), jax.random.fold_in(key_list[1], 1), 0, 1),
        "coeffs": noise(key_list[2], (ORDER, SLAB), (ORDER * 2 // 5) ** -0.5, 0.0390625, ((0, 16), (1, 8))),
        "order": draw_order(jax.random.fold_in(key_list[4], 71), 0),
    }


HIGHEST_PRECISION = lax.Precision.HIGHEST

def orthonormal(tall_matrix):
    gram_matrix = jnp.dot(tall_matrix.T, tall_matrix, precision=HIGHEST_PRECISION)
    lower_factor = jnp.linalg.cholesky(gram_matrix)
    return jax.scipy.linalg.solve_triangular(lower_factor, tall_matrix.T, lower=True).T

def reference(fock, pattern, coeffs, order):
    row_blocks = SLAB // BLK
    col_blocks = ORDER // BLK
    occupied = pattern.astype(jnp.bfloat16)[:, None, :, None]
    masked = (fock.reshape(row_blocks, BLK, col_blocks, BLK) * occupied).reshape(SLAB, ORDER)
    piece_width = min(ORDER, 4096)

    def accumulate(running, position):
        start = (position * piece_width).astype(jnp.int32)
        left_part = lax.dynamic_slice_in_dim(masked, start, piece_width, 1).astype(jnp.float32)
        right_part = lax.dynamic_slice_in_dim(coeffs, start, piece_width, 0).astype(jnp.float32)
        return (running + jnp.dot(left_part, right_part, precision=HIGHEST_PRECISION), None)
    product, _ = lax.scan(accumulate, jnp.zeros((SLAB, SLAB), jnp.float32), jnp.arange(ORDER // piece_width, dtype=jnp.int32))
    matrix = jnp.zeros((row_blocks, BLK, SLAB), jnp.float32).at[order].set(product.reshape(row_blocks, BLK, SLAB)).reshape(SLAB, SLAB)
    panel_rows = matrix[NB:, :NB]
    reflector = orthonormal(orthonormal(panel_rows))
    padded = jnp.concatenate([jnp.zeros((NB, NB), jnp.float32), reflector], axis=0)
    image_cols = jnp.dot(matrix, padded, precision=HIGHEST_PRECISION)
    left_rows = jnp.dot(padded.T, matrix, precision=HIGHEST_PRECISION)
    core_block = jnp.dot(padded.T, image_cols, precision=HIGHEST_PRECISION)
    result = matrix - 2.0 * jnp.dot(padded, left_rows, precision=HIGHEST_PRECISION) - 2.0 * jnp.dot(image_cols, padded.T, precision=HIGHEST_PRECISION) + 4.0 * jnp.dot(padded, jnp.dot(core_block, padded.T, precision=HIGHEST_PRECISION), precision=HIGHEST_PRECISION)
    return result.reshape(SLAB // (NB * GRID_ROWS), GRID_ROWS * NB, SLAB)
```

```python
import jax
import jax.numpy as jnp
from jax import lax
from jax.sharding import PartitionSpec as P

BLK = 64
NB = 256
AXES = ("row", "col")
HIGHEST_PRECISION = lax.Precision.HIGHEST


def locate(index):
    row, col = divmod(index, 16)
    z, y_lo = divmod(row, 2)
    y_hi, rest = divmod(col, 8)
    x, core = divmod(rest, 2)
    return x, y_hi * 2 + y_lo, z, core


def index_of(x, y, z, core):
    y_hi, y_lo = divmod(y, 2)
    return (z % 4 * 2 + y_lo) * 16 + y_hi * 8 + x % 4 * 2 + core


def moves(step, only=lambda x, y, z, core: True):
    return [(i, index_of(*step(*locate(i)))) for i in range(128) if only(*locate(i))]


MOVES = {
    "core": moves(lambda x, y, z, core: (x, y, z, 1 - core)),
    "y_lo": moves(lambda x, y, z, core: (x, y ^ 1, z, core)),
    "y_hi": moves(lambda x, y, z, core: (x, y ^ 2, z, core)),
    "z_up": moves(lambda x, y, z, core: (x, y, z + 1, core)),
    "z_down": moves(lambda x, y, z, core: (x, y, z + 3, core)),
    "z_far": moves(lambda x, y, z, core: (x, y, z + 2, core)),
    "z_a": moves(lambda x, y, z, core: (x, y, z ^ 1, core)),
    "z_b": moves(lambda x, y, z, core: (x, y, z ^ 3, core)),
    "x_a": moves(lambda x, y, z, core: (x ^ 1, y, z, core)),
    "x_b": moves(lambda x, y, z, core: (x ^ 3, y, z, core)),
    "turn": moves(
        lambda x, y, z, core: (z, y, x, core),
        lambda x, y, z, core: core == y % 2,
    ),
}


def deal(high, low):
    def step(x, y, z, core):
        return (z // 2 ^ high) * 2 + y % 2, y // 2 * 2 + core, x, z % 2 ^ low
    return moves(step)


def send(value, move):
    return lax.ppermute(value, AXES, MOVES[move] if isinstance(move, str) else move)


def pick(value, index, axis=0):
    return lax.dynamic_index_in_dim(value, index, axis, keepdims=False)


def total(value, *steps):
    for step in steps:
        value = value + send(value, step)
    return value


def mm(a, b):
    return jnp.dot(a, b, precision=HIGHEST_PRECISION)


def inverse_factor(gram):
    lower = jnp.linalg.cholesky(gram)
    return jax.scipy.linalg.solve_triangular(lower, jnp.eye(NB, dtype=jnp.float32), lower=True).T


def body(fock, pattern, coeffs, order):
    row = lax.axis_index("row")
    col = lax.axis_index("col")
    z, y_lo = row // 2, row % 2
    y_hi, x, core = col // 8, col // 2 % 4, col % 2
    depth = fock.shape[1]

    spread = (jnp.arange(depth)[None, :] // BLK == jnp.arange(depth // BLK)[:, None]).astype(jnp.bfloat16)
    occupied = jnp.dot(pattern.astype(jnp.bfloat16), spread).astype(jnp.bfloat16)
    fock = fock.reshape(4, 2, BLK, depth)
    occupied = occupied.reshape(4, 2, 1, depth)

    def masked_half(which):
        return (pick(fock, which, 1) * pick(occupied, which, 1)).reshape(4 * BLK, depth)

    own = jnp.concatenate([masked_half(1 - core), masked_half(core)], axis=0)
    peer = send(own, "y_lo")
    rows_given = jnp.concatenate([own[: 4 * BLK], peer[: 4 * BLK]], axis=0)
    rows_kept = jnp.concatenate([own[4 * BLK :], peer[4 * BLK :]], axis=0)

    def gather_columns(part):
        above = send(part, "z_down")
        below = send(part, "z_up")
        far_top = send(above[: depth // 2], "z_down")
        far_bottom = send(below[depth // 2 :], "z_up")
        far = jnp.concatenate([far_top, far_bottom], axis=0)
        return jnp.concatenate([part, above, far, below], axis=1)

    def product(columns):
        given = jnp.dot(rows_given, columns, preferred_element_type=jnp.float32)
        kept = jnp.dot(rows_kept, columns, preferred_element_type=jnp.float32)
        return (kept + send(given, "core")).reshape(2, 4, BLK, 4, NB)

    def pair(value, first, second):
        return jnp.stack([pick(value, first), pick(value, second)])

    def reduce_columns(part):
        one, two = part[0], part[1]
        one = pair(one, x, x ^ 3) + send(pair(one, x ^ 1, x ^ 2), "x_a")
        two = pair(two, x, x ^ 1) + send(pair(two, x ^ 3, x ^ 2), "x_b")
        one = one[0] + send(one[1], "x_b")
        two = two[0] + send(two[1], "x_a")
        both = jnp.stack([one, two])

        def side(which):
            return jnp.stack([pick(both, (2 * which + i - z) % 4, 2) for i in range(2)], axis=2)

        return side(y_hi) + send(side(1 - y_hi), "y_hi")

    parts = []
    for j in range(2):
        parts.append(reduce_columns(product(gather_columns(coeffs[:, j * NB : (j + 1) * NB]))))

    order = order.reshape(8, 8)
    piece = parts[0][:, :, 0, :]
    piece = jnp.where(y_hi == 0, piece, send(piece, "y_hi"))
    piece = jnp.where(y_lo == 0, piece, send(piece, "y_lo"))
    atoms_here = pick(order, 2 * x + core, 1)
    piece_atoms = lax.dynamic_slice_in_dim(atoms_here, 2 * z, 2, 0)
    piece = piece * (piece_atoms >= NB // BLK).astype(jnp.float32)[:, None, None]
    flat = piece.reshape(2 * BLK, NB)
    plane = ("core", "x_a", "x_b", "z_a", "z_b")
    first = inverse_factor(total(mm(flat.T, flat), *plane))
    flat = mm(flat, first)
    second = inverse_factor(total(mm(flat.T, flat), *plane))
    factor = mm(first, second)

    slots = jnp.arange(8, dtype=jnp.int32)

    def source_of_slot(atoms):
        target = atoms // 32 * 4 + atoms % 4
        return jnp.sum((target[None, :] == slots[:, None]).astype(jnp.int32) * slots[None, :], axis=1)

    ring = jnp.stack([piece, send(piece, "z_down"), send(piece, "z_far"), send(piece, "z_up")]).reshape(8, BLK, NB)
    source = source_of_slot(atoms_here)
    tiles = jnp.take(ring, (source // 2 - z) % 4 * 2 + source % 2, axis=0).reshape(2, NB, NB)
    panel_cols = pick(tiles, y_hi)
    panel_rows = send(tiles.reshape(2 * NB, NB), "turn")
    panel_rows = jnp.where(core == y_lo, panel_rows, send(panel_rows, "core"))

    both = jnp.stack(parts)
    arrived = []
    for high in range(2):
        for low in range(2):
            chosen = pick(pick(both, z % 2 ^ low), z // 2 ^ high, 2)
            arrived.append(send(chosen, deal(high, low)))
    arrived = jnp.stack(arrived).reshape(8, BLK, NB)
    source = source_of_slot(pick(order, row, 1))
    z_from, y_from = source // 2, source % 2
    turn = ((x // 2) ^ (z_from // 2)) * 2 + (core ^ (z_from % 2))
    matrix = jnp.take(arrived, turn * 2 + (y_from ^ (x % 2)), axis=0).reshape(2 * NB, NB)

    left = total(mm(panel_rows.T, matrix), "z_a", "z_b", "y_lo")
    image = total(mm(matrix, panel_cols), "core", "x_a", "x_b", "y_hi")
    centre = total(mm(panel_rows.T, image), "z_a", "z_b", "y_lo")

    left = mm(factor.T, left)
    image = mm(image, factor)
    centre = mm(mm(factor.T, centre), factor)
    basis_rows = mm(panel_rows, factor)
    basis_cols = mm(panel_cols, factor)
    updated = (
        matrix
        - 2.0 * mm(basis_rows, left - mm(centre, basis_cols.T))
        - 2.0 * mm(image - mm(basis_rows, centre), basis_cols.T)
    )
    return updated.reshape(2, NB, NB)


def solution(mesh):
    return jax.shard_map(
        body,
        mesh=mesh,
        in_specs=(P("row", "col"), P("row", "col"), P("col", "row"), P()),
        out_specs=P(None, "row", "col"),
        check_vma=False,
    )
```

```python
import functools

import jax
import jax.numpy as jnp
from jax import lax
from jax.experimental import pallas as pl
from jax.experimental.pallas import tpu as pltpu
from jax.sharding import PartitionSpec as P

BLK = 64
NB = 256
AXES = ("row", "col")
HIGHEST_PRECISION = lax.Precision.HIGHEST


def locate(index):
    row, col = divmod(index, 16)
    z, y_lo = divmod(row, 2)
    y_hi, rest = divmod(col, 8)
    x, core = divmod(rest, 2)
    return x, y_hi * 2 + y_lo, z, core


def index_of(x, y, z, core):
    y_hi, y_lo = divmod(y, 2)
    return (z % 4 * 2 + y_lo) * 16 + y_hi * 8 + x % 4 * 2 + core


def moves(step, only=lambda x, y, z, core: True):
    return [(i, index_of(*step(*locate(i)))) for i in range(128) if only(*locate(i))]


MOVES = {
    "core": moves(lambda x, y, z, core: (x, y, z, 1 - core)),
    "y_lo": moves(lambda x, y, z, core: (x, y ^ 1, z, core)),
    "y_hi": moves(lambda x, y, z, core: (x, y ^ 2, z, core)),
    "z_far": moves(lambda x, y, z, core: (x, y, z + 2, core)),
    "z_a": moves(lambda x, y, z, core: (x, y, z ^ 1, core)),
    "z_b": moves(lambda x, y, z, core: (x, y, z ^ 3, core)),
    "x_far": moves(lambda x, y, z, core: (x ^ 2, y, z, core)),
    "x_a": moves(lambda x, y, z, core: (x ^ 1, y, z, core)),
    "x_b": moves(lambda x, y, z, core: (x ^ 3, y, z, core)),
    "turn": moves(
        lambda x, y, z, core: (z, y, x, core),
        lambda x, y, z, core: core == y % 2,
    ),
}


def deal(e, low):
    def step(x, y, z, core):
        return (z % 2 ^ e) * 2 + y % 2, y // 2 * 2 + core, x, z // 2 ^ low
    return moves(step)


def send(value, move):
    return lax.ppermute(value, AXES, MOVES[move] if isinstance(move, str) else move)


def pick(value, index, axis=0):
    return lax.dynamic_index_in_dim(value, index, axis, keepdims=False)


def total(value, *steps):
    for step in steps:
        value = value + send(value, step)
    return value


def after(value, *earlier):
    return lax.optimization_barrier((value, *earlier))[0]


def mm(a, b, precision=lax.Precision.HIGH):
    return jnp.dot(a, b, precision=precision)


def is_same(shape, scale=1):
    rows = lax.broadcasted_iota(jnp.int32, shape, 0)
    return rows == lax.broadcasted_iota(jnp.int32, shape, 1) // scale


def mask_kernel(places, fock, pattern, out, spread):
    @pl.when(pl.program_id(0) == 0)
    def _():
        same = is_same(spread.shape, BLK).astype(jnp.float32)
        spread[...] = same.astype(jnp.bfloat16)
    row = pattern[pl.ds(places[pl.program_id(0)], 1), :].astype(jnp.float32).astype(jnp.bfloat16)
    row = jnp.broadcast_to(row, (16, row.shape[1]))
    wide = jnp.dot(row, spread[...], preferred_element_type=jnp.float32).astype(jnp.bfloat16)
    out[0] = fock[0] * jnp.broadcast_to(wide[0:1], fock.shape[1:])


def masked_rows(fock, pattern, places):
    blocks, depth = pattern.shape[0], fock.shape[1]
    return pl.pallas_call(
        mask_kernel,
        grid_spec=pltpu.PrefetchScalarGridSpec(
            num_scalar_prefetch=1,
            grid=(blocks,),
            in_specs=[
                pl.BlockSpec((1, BLK, depth), lambda i, places: (places[i], 0, 0)),
                pl.BlockSpec(pattern.shape, lambda i, places: (0, 0)),
            ],
            out_specs=pl.BlockSpec((1, BLK, depth), lambda i, places: (i, 0, 0)),
            scratch_shapes=[pltpu.VMEM((pattern.shape[1], depth), jnp.bfloat16)],
        ),
        out_shape=jax.ShapeDtypeStruct((blocks, BLK, depth), jnp.bfloat16),
        cost_estimate=pl.CostEstimate(flops=10**8, bytes_accessed=4 * fock.size, transcendentals=0),
        compiler_params=pltpu.CompilerParams(vmem_limit_bytes=32 * 2**20),
        name="mask",
    )(places, fock.reshape(blocks, BLK, depth), pattern).reshape(fock.shape)


def product_kernel(steps, own, peer, c0, c1, c2_top, c2_bottom, c3, out):
    k = pl.program_id(0)
    width = c0.shape[1]
    rows = jnp.concatenate([own[...], peer[...]], axis=0)
    c2 = jnp.where(k < steps // 2, c2_top[...], c2_bottom[...])
    columns = jnp.concatenate([c0[...], c1[...], c2, c3[...]], axis=1)

    def tiles():
        for start in range(0, 4 * width, NB):
            tile = jnp.dot(rows, columns[:, start : start + NB], preferred_element_type=jnp.float32)
            for lo in range(start, start + NB, 128):
                yield lo // width, slice(lo % width, lo % width + 128), tile[:, lo - start : lo - start + 128]

    @pl.when(k == 0)
    def _():
        for e, where, tile in tiles():
            out[e, :, where] = tile

    @pl.when(k > 0)
    def _():
        for e, where, tile in tiles():
            out[e, :, where] += tile


def product(half, own, peer, c0, c1, c2_top, c2_bottom, c3):
    depth, width = c0.shape
    tall = own.shape[0] // 2
    steps = 4
    deep = depth // steps
    rows = pl.BlockSpec((tall, deep), lambda k: (half, k))
    columns = pl.BlockSpec((deep, width), lambda k: (k, 0))
    top = pl.BlockSpec((deep, width), lambda k: (jnp.minimum(k, steps // 2 - 1), 0))
    bottom = pl.BlockSpec((deep, width), lambda k: (jnp.maximum(k - steps // 2, 0), 0))
    out = pl.pallas_call(
        functools.partial(product_kernel, steps),
        grid=(steps,),
        in_specs=[rows, rows, columns, columns, top, bottom, columns],
        out_specs=pl.BlockSpec((4, 2 * tall, width), lambda k: (0, 0, 0)),
        out_shape=jax.ShapeDtypeStruct((4, 2 * tall, width), jnp.float32),
        cost_estimate=pl.CostEstimate(
            flops=2 * 2 * tall * 4 * width * depth,
            bytes_accessed=2 * depth * (2 * tall + 4 * width) + 32 * tall * width,
            transcendentals=0,
        ),
        compiler_params=pltpu.CompilerParams(vmem_limit_bytes=48 * 2**20),
        name="product",
    )(own, peer, c0, c1, c2_top, c2_bottom, c3)
    return out.reshape(4, 2, 4, BLK, width)


def panel_kernel(steps, piece, own, peer, c0, c1, c2_top, c2_bottom, c3, out):
    k = pl.program_id(0)

    @pl.when(k == 0)
    def _():
        out[...] = jnp.zeros_like(out)

    def add(columns):
        rows = jnp.concatenate([own[...], peer[...]], axis=0)
        out[...] += jnp.dot(rows, columns[...], preferred_element_type=jnp.float32)

    for e, columns in ((0, c0), (1, c1), (3, c3)):
        pl.when(piece[0] == e)(functools.partial(add, columns))
    pl.when((piece[0] == 2) & (k < steps // 2))(functools.partial(add, c2_top))
    pl.when((piece[0] == 2) & (k >= steps // 2))(functools.partial(add, c2_bottom))


def panel_product(piece, own, peer, c0, c1, c2_top, c2_bottom, c3):
    depth = c0.shape[0]
    tall = own.shape[0]
    steps = 4
    deep = depth // steps
    rows = pl.BlockSpec((tall, deep), lambda k, piece: (0, k))

    def columns(e, step):
        return pl.BlockSpec((deep, NB), lambda k, piece: (jnp.where(piece[0] == e, step(k), 0), 0))

    out = pl.pallas_call(
        functools.partial(panel_kernel, steps),
        grid_spec=pltpu.PrefetchScalarGridSpec(
            num_scalar_prefetch=1,
            grid=(steps,),
            in_specs=[
                rows,
                rows,
                columns(0, lambda k: k),
                columns(1, lambda k: k),
                columns(2, lambda k: jnp.minimum(k, steps // 2 - 1)),
                columns(2, lambda k: jnp.maximum(k - steps // 2, 0)),
                columns(3, lambda k: k),
            ],
            out_specs=pl.BlockSpec((2 * tall, NB), lambda k, piece: (0, 0)),
        ),
        out_shape=jax.ShapeDtypeStruct((2 * tall, NB), jnp.float32),
        cost_estimate=pl.CostEstimate(
            flops=4 * tall * NB * depth, bytes_accessed=2 * depth * (2 * tall + NB) + 8 * tall * NB, transcendentals=0
        ),
        compiler_params=pltpu.CompilerParams(vmem_limit_bytes=48 * 2**20),
        name="panel_product",
    )(piece.reshape(1), own, peer, c0, c1, c2_top, c2_bottom, c3)
    return out.reshape(2, 2, 4, BLK, NB)


def eliminate(block, group):
    size = block.shape[0]
    same = is_same((size, size)).astype(jnp.float32)
    work = jnp.concatenate([block, same], axis=1)
    row = lax.broadcasted_iota(jnp.int32, work.shape, 0)
    for start in range(0, size, group):
        columns = [jnp.broadcast_to(work[:, start + i : start + i + 1], work.shape) for i in range(group)]
        for i in range(group):
            at = start + i
            if at == size - 1:
                break
            share = jnp.where(row > at, columns[i] * (1.0 / columns[i][at : at + 1]), 0.0)
            for k in range(i + 1, group):
                columns[k] = columns[k] - share * columns[k][at : at + 1]
            work = work - share * work[at : at + 1]
    pivots = jnp.sum(work[:, :size] * same, axis=1, keepdims=True)
    return work[:, size:] * lax.rsqrt(pivots)


def inverse_kernel(size, gram, out, rest):
    f32_dot = functools.partial(jnp.dot, precision=HIGHEST_PRECISION, preferred_element_type=jnp.float32)
    rest[...] = gram[...]
    out[...] = is_same(out.shape).astype(jnp.float32)
    for lo in range(0, NB, size):
        hi = lo + size
        inverse = eliminate(rest[lo:hi, lo:hi], 16)
        factor = f32_dot(inverse, rest[lo:hi, :])
        done = f32_dot(inverse, out[lo:hi, :])
        out[lo:hi, :] = done
        if hi < NB:
            below = factor.T[hi:, :]
            rest[hi:, :] -= f32_dot(below, factor)
            out[hi:, :] -= f32_dot(below, done)


def inverse_factor(gram):
    return pl.pallas_call(
        functools.partial(inverse_kernel, 64),
        out_shape=jax.ShapeDtypeStruct((NB, NB), jnp.float32),
        scratch_shapes=[pltpu.VMEM((NB, NB), jnp.float32)],
        cost_estimate=pl.CostEstimate(flops=10**10, bytes_accessed=2**19, transcendentals=0),
        compiler_params=pltpu.CompilerParams(vmem_limit_bytes=16 * 2**20),
        name="inverse_factor",
    )(gram)


class Rounds:
    def __init__(self):
        self.last = ()

    def open(self, *values):
        values = lax.optimization_barrier((*values, *self.last))[: len(values)]
        return values[0] if len(values) == 1 else values

    def close(self, *results):
        self.last = results


def body(fock, pattern, coeffs, order):
    row = lax.axis_index("row")
    col = lax.axis_index("col")
    z, y_lo = row // 2, row % 2
    y_hi, x, core = col // 8, col // 2 % 4, col % 2
    x_high, z_high, z_low = x // 2, z // 2, z % 2
    depth = fock.shape[1]
    half = depth // 2
    order = order.reshape(8, 8)
    rounds = Rounds()

    slots = jnp.arange(8, dtype=jnp.int32)

    def source_of_slot(atoms):
        target = atoms // 32 * 4 + atoms % 4
        return jnp.sum((target[None, :] == slots[:, None]).astype(jnp.int32) * slots[None, :], axis=1)

    atoms_here = pick(order, 2 * x + core, 1)
    piece_atoms = lax.dynamic_slice_in_dim(atoms_here, 2 * z, 2, 0)
    trailing = (piece_atoms >= NB // BLK).astype(jnp.float32)[:, None, None]
    here = source_of_slot(atoms_here)
    here = ((here // 2) ^ z) * 2 + here % 2
    source = source_of_slot(pick(order, row, 1))
    z_from, y_from = source // 2, source % 2
    dealt = (((x // 2) ^ (z_from % 2)) * 2 + (core ^ (z_from // 2))) * 2 + (y_from ^ (x % 2))

    def in_order(value):
        return jnp.take(value.reshape(8, BLK, NB), here, axis=0).reshape(2 * NB, NB)

    def halves_of_gram(a, b, precision):
        mine = mm(lax.dynamic_slice_in_dim(a, core * (NB // 2), NB // 2, 1).T, b, precision)
        others = mm(lax.dynamic_slice_in_dim(a, (1 - core) * (NB // 2), NB // 2, 1).T, b, precision)
        return mine, others

    def send_over_x(value):
        return send(value, "x_a"), send(value, "x_far"), send(value, "x_b")

    def whole(mine, others):
        return jnp.where(core == 0, jnp.concatenate([mine, others]), jnp.concatenate([others, mine]))

    def bulk_first(value):
        one, two = value[:, 0], value[:, 1]
        return (
            (one, send(jnp.stack([one[:, 1], one[:, 2]]), "x_a")),
            (two, send(jnp.stack([two[:, 3], two[:, 2]]), "x_b")),
        )

    def bulk_second(first):
        (one, got_one), (two, got_two) = first
        one = jnp.stack([one[:, 0], one[:, 3]]) + got_one
        two = jnp.stack([two[:, 0], two[:, 1]]) + got_two
        return (one[0], send(one[1], "x_b")), (two[0], send(two[1], "x_a"))

    def bulk_third(second):
        (one, got_one), (two, got_two) = second
        both = jnp.stack([one + got_one, two + got_two], axis=1)
        both = both.reshape(2, 2, *both.shape[1:])
        return pick(both, z_high ^ y_hi), send(pick(both, z_high ^ y_hi ^ 1), "y_hi")

    wide = depth * 3 // 32
    c0 = coeffs[:, :wide]
    a0, b0 = send(c0, "z_a"), send(c0, "z_b")
    e = jnp.arange(4, dtype=jnp.int32)
    places = jnp.concatenate([2 * (x ^ e) + 1 - core, 2 * (x ^ e) + core])
    own = masked_rows(fock, pattern, places)
    peer = send(own, "y_lo")
    c1 = after(coeffs[:, wide:], a0, b0)
    f0, g0 = send(b0[:half], "z_a"), send(a0[half:], "z_b")
    a1, b1 = send(c1, "z_a"), send(c1, "z_b")

    panel = panel_product(z, own, peer, c0, a0, f0, g0, b0)
    got = send(panel[:, 0], "core")
    rounds.close(got)
    panel, own_2 = rounds.open(panel, own)
    panel = panel[:, 1] + got
    t1, t2, t3 = send(panel[:, 1], "x_a"), send(panel[:, 2], "x_far"), send(panel[:, 3], "x_b")
    given = product(0, own_2, peer, c0, a0, f0, g0, b0)
    rounds.close(t1, t2, t3, given)
    panel, own_3, given = rounds.open(panel, own, given)
    piece = (panel[:, 0] + t1) + (t2 + t3)
    got_piece = send(piece, "y_hi")
    got = send(given, "core")
    kept = product(1, own_3, peer, c0, a0, f0, g0, b0)
    rounds.close(got_piece, got, kept)
    piece, kept, a1_4, b1_4 = rounds.open(piece, kept, a1, b1)
    f1, g1 = send(b1_4[:half], "z_a"), send(a1_4[half:], "z_b")
    piece = piece + got_piece
    got_piece = send(piece, "y_lo")
    first = bulk_first((kept + got).reshape(4, 2, 4, BLK, wide))
    rounds.close(got_piece)
    piece = rounds.open(piece)
    piece = jnp.where(y_lo == 0, piece, got_piece) * trailing
    got_piece = send(piece, "z_a")
    rounds.close(got_piece)
    piece = rounds.open(piece)
    ring = jnp.stack([piece, got_piece])
    got_ring = send(ring, "z_b")
    rounds.close(got_ring)
    ring = rounds.open(ring)
    ring = jnp.concatenate([ring, got_ring[::-1]]).reshape(2 * NB, NB)
    mine, others = halves_of_gram(ring, ring, HIGHEST_PRECISION)
    got = send(others, "core")
    second = bulk_second(first)
    tiles = in_order(ring)
    panel_cols = pick(tiles.reshape(2, NB, NB), y_hi)
    rounds.close(got, tiles, panel_cols)
    mine = rounds.open(mine) + got
    t1, t2, t3 = send_over_x(mine)
    given = product(0, own, peer, c1, a1, f1, g1, b1)
    rounds.close(t1, t2, t3, given)
    mine, own_9, given, panel_cols = rounds.open(mine, own, given, panel_cols)
    mine = (mine + t1) + (t2 + t3)
    others = send(mine, "core")
    got = send(given, "core")
    kept = product(1, own_9, peer, c1, a1, f1, g1, b1)
    near = send(panel_cols, "x_a")
    rounds.close(others, got, kept, near, second[0][1], second[1][1])
    mine, kept, tiles = rounds.open(mine, kept, tiles)
    first = bulk_first((kept + got).reshape(4, 2, 4, BLK, depth // 8 - wide))
    third = bulk_third(second)
    turned = send(tiles, "turn")
    tile = jnp.where(x % 2 == y_lo, panel_cols, near)
    tile_far = send(tile, "x_far")
    factor_1 = inverse_factor(whole(mine, others))
    rounds.close(factor_1, third[1], first[0][1], first[1][1], tile_far)
    factor_1, tile = rounds.open(factor_1, tile)
    once = mm(ring, factor_1.T, HIGHEST_PRECISION)
    mine, others = halves_of_gram(once, once, HIGHEST_PRECISION)
    got = send(others, "core")
    second = bulk_second(first)
    tile = jnp.stack([tile, tile_far])
    tile_core = send(tile, "core")
    rounds.close(got, tile_core)
    mine, turned = rounds.open(mine, turned)
    mine = mine + got
    t1, t2, t3 = send_over_x(mine)
    turned_core = send(turned, "core")
    rounds.close(t1, t2, t3, turned_core, second[0][1], second[1][1])
    mine, turned = rounds.open(mine, turned)
    mine = (mine + t1) + (t2 + t3)
    others = send(mine, "core")
    last = bulk_third(second)
    panel_rows = jnp.where(core == y_lo, turned, turned_core)
    rounds.close(others, last[1])
    mine, tile = rounds.open(mine, tile)
    both = jnp.concatenate([third[0] + third[1], last[0] + last[1]], axis=-1)
    tile = jnp.stack([tile, tile_core])
    image = 0.0
    for side in range(2):
        for j in range(2):
            block = both[side, :, :, j * NB : (j + 1) * NB].reshape(2 * BLK, NB)
            image = image + mm(block, pick(pick(tile, core ^ j), x_high ^ z_low ^ side))
    image = image.reshape(2, BLK, NB)
    image = jnp.where(y_lo == 0, image, image[::-1])
    got_image = send(image, "y_hi")
    arrived = []
    for side in range(2):
        for low in range(2):
            piece = lax.dynamic_slice_in_dim(both[side], (z_high ^ low) * NB, NB, 2)
            arrived.append(send(piece, deal(side, low)))
    factor_2 = inverse_factor(whole(mine, others))
    rounds.close(got_image, factor_2, *arrived)
    image, factor_2, *arrived = rounds.open(image, factor_2, *arrived)
    image = image + got_image
    got_image = send(image, "y_lo")
    matrix = jnp.take(jnp.stack(arrived).reshape(8, BLK, NB), dealt, axis=0).reshape(2 * NB, NB)
    left = mm(panel_rows.T, matrix)
    got_left = send(left, "z_a")
    factor = mm(factor_2, factor_1, HIGHEST_PRECISION).T
    rounds.close(got_image, got_left, factor)
    image, left = rounds.open(image, left)
    image = image + got_image
    left = left + got_left
    image = jnp.stack([image, send(image, "z_a"), send(image, "z_far"), send(image, "z_b")]).reshape(2 * NB, NB)
    got_left = send(left, "z_b")
    rounds.close(image, got_left)
    image, left = rounds.open(image, left)
    left = left + got_left
    mine, others = halves_of_gram(ring, image, lax.Precision.HIGH)
    got = send(others, "core")
    turned = send(in_order(image), "turn")
    got_left = send(left, "y_lo")
    rounds.close(got)
    mine = rounds.open(mine) + got
    t1, t2, t3 = send_over_x(mine)
    rounds.close(t1, t2, t3, got_left)
    mine, turned = rounds.open(mine, turned)
    mine = (mine + t1) + (t2 + t3)
    others = send(mine, "core")
    turned_core = send(turned, "core")
    centre = whole(mine, others)
    image = jnp.where(core == y_lo, turned, turned_core)
    left = left + got_left

    left = mm(factor.T, left)
    image = mm(image, factor)
    centre = mm(mm(factor.T, centre), factor)
    basis_rows = mm(panel_rows, factor)
    basis_cols = mm(panel_cols, factor)
    updated = (
        matrix
        - 2.0 * mm(basis_rows, left - mm(centre, basis_cols.T))
        - 2.0 * mm(image - mm(basis_rows, centre), basis_cols.T)
    )
    return updated.reshape(2, NB, NB)


def solution(mesh):
    return jax.shard_map(
        body,
        mesh=mesh,
        in_specs=(P("row", "col"), P("row", "col"), P("col", "row"), P()),
        out_specs=P(None, "row", "col"),
        check_vma=False,
    )
```

```python
import functools

import jax
import jax.numpy as jnp
from jax import lax
from jax.experimental import pallas as pl
from jax.experimental.pallas import tpu as pltpu
from jax.sharding import PartitionSpec as P

BLK = 64
NB = 256
AXES = ("row", "col")
HIGHEST_PRECISION = lax.Precision.HIGHEST


def locate(index):
    row, col = divmod(index, 16)
    z, y_lo = divmod(row, 2)
    y_hi, rest = divmod(col, 8)
    x, core = divmod(rest, 2)
    return x, y_hi * 2 + y_lo, z, core


def index_of(x, y, z, core):
    y_hi, y_lo = divmod(y, 2)
    return (z % 4 * 2 + y_lo) * 16 + y_hi * 8 + x % 4 * 2 + core


def moves(step, only=lambda x, y, z, core: True):
    return [(i, index_of(*step(*locate(i)))) for i in range(128) if only(*locate(i))]


MOVES = {
    "core": moves(lambda x, y, z, core: (x, y, z, 1 - core)),
    "y_lo": moves(lambda x, y, z, core: (x, y ^ 1, z, core)),
    "y_hi": moves(lambda x, y, z, core: (x, y ^ 2, z, core)),
    "y_both": moves(lambda x, y, z, core: (x, y ^ 3, z, core)),
    "z_far": moves(lambda x, y, z, core: (x, y, z + 2, core)),
    "z_a": moves(lambda x, y, z, core: (x, y, z ^ 1, core)),
    "z_b": moves(lambda x, y, z, core: (x, y, z ^ 3, core)),
    "x_far": moves(lambda x, y, z, core: (x ^ 2, y, z, core)),
    "x_a": moves(lambda x, y, z, core: (x ^ 1, y, z, core)),
    "x_b": moves(lambda x, y, z, core: (x ^ 3, y, z, core)),
}


def deal(e, low):
    def step(x, y, z, core):
        return (z % 2 ^ e) * 2 + y % 2, y // 2 * 2 + core, x, z // 2 ^ low
    return moves(step)


def send(value, move):
    return lax.ppermute(value, AXES, MOVES[move] if isinstance(move, str) else move)


def pick(value, index, axis=0):
    return lax.dynamic_index_in_dim(value, index, axis, keepdims=False)


def total(value, *steps):
    for step in steps:
        value = value + send(value, step)
    return value


def after(value, *earlier):
    return lax.optimization_barrier((value, *earlier))[0]


def mm(a, b, precision=lax.Precision.HIGH):
    return jnp.dot(a, b, precision=precision)


def is_same(shape, scale=1):
    rows = lax.broadcasted_iota(jnp.int32, shape, 0)
    return rows == lax.broadcasted_iota(jnp.int32, shape, 1) // scale


def mask_kernel(places, fock, pattern, out, spread):
    @pl.when(pl.program_id(0) == 0)
    def _():
        same = is_same(spread.shape, BLK).astype(jnp.float32)
        spread[...] = same.astype(jnp.bfloat16)
    row = pattern[pl.ds(places[pl.program_id(0)], 1), :].astype(jnp.float32).astype(jnp.bfloat16)
    row = jnp.broadcast_to(row, (16, row.shape[1]))
    wide = jnp.dot(row, spread[...], preferred_element_type=jnp.float32).astype(jnp.bfloat16)
    out[0] = fock[0] * jnp.broadcast_to(wide[0:1], fock.shape[1:])


def masked_rows(fock, pattern, places):
    blocks, depth = pattern.shape[0], fock.shape[1]
    return pl.pallas_call(
        mask_kernel,
        grid_spec=pltpu.PrefetchScalarGridSpec(
            num_scalar_prefetch=1,
            grid=(blocks,),
            in_specs=[
                pl.BlockSpec((1, BLK, depth), lambda i, places: (places[i], 0, 0)),
                pl.BlockSpec(pattern.shape, lambda i, places: (0, 0)),
            ],
            out_specs=pl.BlockSpec((1, BLK, depth), lambda i, places: (i, 0, 0)),
            scratch_shapes=[pltpu.VMEM((pattern.shape[1], depth), jnp.bfloat16)],
        ),
        out_shape=jax.ShapeDtypeStruct((blocks, BLK, depth), jnp.bfloat16),
        cost_estimate=pl.CostEstimate(flops=10**8, bytes_accessed=4 * fock.size, transcendentals=0),
        compiler_params=pltpu.CompilerParams(vmem_limit_bytes=32 * 2**20),
        name="mask",
    )(places, fock.reshape(blocks, BLK, depth), pattern).reshape(fock.shape)


def eliminate(block, group):
    size = block.shape[0]
    same = is_same((size, size)).astype(jnp.float32)
    work = jnp.concatenate([block, same], axis=1)
    row = lax.broadcasted_iota(jnp.int32, work.shape, 0)
    for start in range(0, size, group):
        columns = [jnp.broadcast_to(work[:, start + i : start + i + 1], work.shape) for i in range(group)]
        for i in range(group):
            at = start + i
            if at == size - 1:
                break
            share = jnp.where(row > at, columns[i] * (1.0 / columns[i][at : at + 1]), 0.0)
            for k in range(i + 1, group):
                columns[k] = columns[k] - share * columns[k][at : at + 1]
            work = work - share * work[at : at + 1]
    pivots = jnp.sum(work[:, :size] * same, axis=1, keepdims=True)
    return work[:, size:] * lax.rsqrt(pivots)


def inverse_kernel(size, gram, out, rest):
    f32_dot = functools.partial(jnp.dot, precision=HIGHEST_PRECISION, preferred_element_type=jnp.float32)
    rest[...] = gram[...]
    out[...] = is_same(out.shape).astype(jnp.float32)
    for lo in range(0, NB, size):
        hi = lo + size
        inverse = eliminate(rest[lo:hi, lo:hi], 16)
        factor = f32_dot(inverse, rest[lo:hi, :])
        done = f32_dot(inverse, out[lo:hi, :])
        out[lo:hi, :] = done
        if hi < NB:
            below = factor.T[hi:, :]
            rest[hi:, :] -= f32_dot(below, factor)
            out[hi:, :] -= f32_dot(below, done)


def inverse_factor(gram):
    return pl.pallas_call(
        functools.partial(inverse_kernel, 64),
        out_shape=jax.ShapeDtypeStruct((NB, NB), jnp.float32),
        scratch_shapes=[pltpu.VMEM((NB, NB), jnp.float32)],
        cost_estimate=pl.CostEstimate(flops=10**10, bytes_accessed=2**19, transcendentals=0),
        compiler_params=pltpu.CompilerParams(vmem_limit_bytes=16 * 2**20),
        name="inverse_factor",
    )(gram)


class Rounds:
    def __init__(self):
        self.last = ()

    def open(self, *values):
        values = lax.optimization_barrier((*values, *self.last))[: len(values)]
        return values[0] if len(values) == 1 else values

    def close(self, *results):
        self.last = results


def body(fock, pattern, coeffs, order):
    row = lax.axis_index("row")
    col = lax.axis_index("col")
    z, y_lo = row // 2, row % 2
    y_hi, x, core = col // 8, col // 2 % 4, col % 2
    z_high, z_low = z // 2, z % 2
    depth = fock.shape[1]
    half = depth // 2
    rounds = Rounds()

    def count(mask, values):
        return jnp.sum(mask.astype(jnp.int32) * values, axis=1)

    slots = jnp.arange(8, dtype=jnp.int32)
    places = jnp.arange(64, dtype=jnp.int32)

    def panel_place(r, s):
        return (((s % 2) ^ core) * 4 + ((s // 2) ^ x)) * 8 + ((r // 2) ^ z) * 2 + r % 2

    def atoms_place(atoms):
        position = count(order[None, :] == atoms[:, None], places[None, :])
        return panel_place(position // 8, position % 8)

    def atoms_of(column_tile):
        return column_tile * 4 + slots[:4]

    row_places = atoms_place((slots // 4 * 8 + row) * 4 + slots % 4)
    dealt_z = 2 * (core ^ (slots // 2 % 2)) + ((x // 2) ^ (slots // 4))
    dealt_places = panel_place(2 * dealt_z + ((slots % 2) ^ (x % 2)), row)
    side_places = [
        atoms_place(atoms_of(y_hi * 8 + (2 * (z_low ^ side) + y_lo) * 2 + j)) for side in range(2) for j in range(2)
    ]
    places_used = jnp.concatenate([row_places, dealt_places, *side_places])
    by_row = order.reshape(8, 8)
    trailing = lax.dynamic_slice_in_dim(pick(by_row, 2 * x + core, 1), 2 * z, 2, 0)
    trailing = (trailing >= NB // BLK).astype(jnp.float32)[:, None, None]
    target = pick(by_row, row, 1)
    target = target // 32 * 4 + target % 4
    source = count(target[None, :] == slots[:, None], slots[None, :])
    z_from, y_from = source // 2, source % 2
    dealt = (((x // 2) ^ (z_from % 2)) * 2 + (core ^ (z_from // 2))) * 2 + (y_from ^ (x % 2))

    def product(columns):
        rows = jnp.concatenate([own, peer], axis=0)
        return jnp.dot(rows, columns, preferred_element_type=jnp.float32).reshape(2, 2, 4, BLK, NB)

    def to_other_core(blocks):
        blocks = jnp.stack(blocks)
        return blocks[:, :, 1], send(blocks[:, :, 0], "core")

    def first_over_x(one, two):
        return (
            (one, send(jnp.stack([one[:, 1], one[:, 2]]), "x_a")),
            (two, send(jnp.stack([two[:, 3], two[:, 2]]), "x_b")),
        )

    def second_over_x(first):
        (one, got_one), (two, got_two) = first
        one = jnp.stack([one[:, 0], one[:, 3]]) + got_one
        two = jnp.stack([two[:, 0], two[:, 1]]) + got_two
        return (one[0], send(one[1], "x_b")), (two[0], send(two[1], "x_a"))

    def sums(second):
        return second[0][0] + second[0][1], second[1][0] + second[1][1]

    def landed(parts):
        return parts[0][1], parts[1][1]

    e = jnp.arange(4, dtype=jnp.int32)
    own = masked_rows(fock, pattern, jnp.concatenate([2 * (x ^ e) + 1 - core, 2 * (x ^ e) + core]))
    peer = send(own, "y_lo")
    c0 = coeffs[:, :NB]
    a0, b0 = send(c0, "z_a"), send(c0, "z_b")
    f0, g0 = send(b0[:half], "z_a"), send(a0[half:], "z_b")
    c1 = after(coeffs[:, NB:], a0, b0)
    a1, b1 = send(c1, "z_a"), send(c1, "z_b")
    f1, g1 = send(b1[:half], "z_a"), send(a1[half:], "z_b")
    rounds.close(peer, f0, g0)

    own, peer = rounds.open(own, peer)
    far = jnp.concatenate([f0, g0], axis=0)
    kept, got = to_other_core([product(columns) for columns in (c0, a0, far, b0)])
    rounds.close(got, a1, b1)
    kept, c1 = rounds.open(kept, c1)
    kept = kept + got
    first = first_over_x(kept[:, 0], kept[:, 1])
    blocks = [product(c1)]
    rounds.close(*landed(first), *blocks)
    a1_now, b1_now = rounds.open(a1, b1)
    second = second_over_x(first)
    blocks += [product(a1_now), product(b1_now)]
    rounds.close(*landed(second), *blocks)
    both = rounds.open(jnp.stack(sums(second), axis=1))
    piece = pick(both, z)
    halves = both.reshape(2, 2, *both.shape[1:])
    got = send(jnp.concatenate([pick(halves, z_high ^ y_hi ^ 1), piece[None]]), "y_hi")
    got_lo, got_both = send(piece, "y_lo"), send(piece, "y_both")
    rounds.close(got, got_lo, got_both, f1, g1)
    piece, halves, f1 = rounds.open(piece, halves, f1)
    first_part = pick(halves, z_high ^ y_hi) + got[:2]
    piece = jnp.where(y_lo == 0, piece + got[2], got_lo + got_both) * trailing
    ring = [piece, send(piece, "z_a"), send(piece, "z_far"), send(piece, "z_b")]
    blocks.insert(2, product(jnp.concatenate([f1, g1], axis=0)))
    kept, got = to_other_core(blocks)
    rounds.close(got, *ring)
    kept, *ring = rounds.open(kept, *ring)
    ring = jnp.stack(ring)
    ring = [ring, send(ring, "x_a"), send(ring, "x_far"), send(ring, "x_b")]
    kept = (kept + got).reshape(2, 2, 2, 4, BLK, NB)
    got = send(pick(kept, z_high ^ y_hi ^ 1), "y_hi")
    kept = pick(kept, z_high ^ y_hi)
    rounds.close(got, *ring)
    kept, *ring = rounds.open(kept, *ring)
    panel = jnp.stack(ring)
    got_panel = send(panel, "core")
    kept = kept + got
    t1, t2, t3 = send(kept[:, :, 1], "x_a"), send(kept[:, :, 2], "x_far"), send(kept[:, :, 3], "x_b")
    rows_here = panel.reshape(8 * NB, NB)
    rows_there = got_panel.reshape(8 * NB, NB)
    factor_1 = inverse_factor(mm(rows_here.T, rows_here) + mm(rows_there.T, rows_there))
    panel = jnp.stack([panel, got_panel])
    tiles = jnp.take(panel.reshape(64, BLK, NB), places_used, axis=0)
    rounds.close(t1, t2, t3, factor_1, tiles)
    last_part, tiles, factor_1 = rounds.open(kept[:, :, 0], tiles, factor_1)
    last_part = (last_part + t1) + (t2 + t3)
    both = jnp.stack([first_part, last_part])
    panel_rows, panel_dealt = tiles[:8].reshape(2 * NB, NB), tiles[8:16].reshape(2 * NB, NB)
    side_tiles = tiles[16:].reshape(2, 2, NB, NB)
    both = both.reshape(2, 2, 2 * BLK, NB)
    image = 0.0
    for side in range(2):
        for j in range(2):
            image = image + mm(both[j, side], side_tiles[side, j])
    image = image.reshape(2, BLK, NB)
    image = jnp.where(y_lo == 0, image, image[::-1])
    got_hi, got_lo, got_both = send(image, "y_hi"), send(image, "y_lo"), send(image, "y_both")
    once_here, once_there = mm(rows_here, factor_1.T), mm(rows_there, factor_1.T)
    factor_2 = inverse_factor(mm(once_here.T, once_here) + mm(once_there.T, once_there))
    rounds.close(got_hi, got_lo, got_both, factor_2)
    image, factor_2, both = rounds.open(image, factor_2, both)
    image = (image + got_hi) + (got_lo + got_both)
    image = jnp.where(y_lo == 0, image, image[::-1]).reshape(2 * BLK, NB)
    factor = mm(factor_2, factor_1, HIGHEST_PRECISION).T
    image = mm(mm(image, factor), factor.T)
    both = jnp.stack(
        [jnp.stack([both[j, side] - 2.0 * mm(image, side_tiles[side, j].T) for side in range(2)]) for j in range(2)]
    )
    arrived = [send(pick(both[:, side], z_high ^ low), deal(side, low)) for side in range(2) for low in range(2)]
    rounds.close(*arrived)
    arrived = rounds.open(*arrived)
    arrived = jnp.stack(arrived).reshape(2 * NB, NB)
    left = total(mm(panel_dealt.T, arrived), "z_a", "z_b", "y_lo")
    matrix = jnp.take(arrived.reshape(8, BLK, NB), dealt, axis=0).reshape(2 * NB, NB)
    rows = mm(mm(panel_rows, factor), factor.T)
    updated = matrix - 2.0 * mm(rows, left)
    return updated.reshape(2, NB, NB)


def solution(mesh):
    return jax.shard_map(
        body,
        mesh=mesh,
        in_specs=(P("row", "col"), P("row", "col"), P("col", "row"), P()),
        out_specs=P(None, "row", "col"),
        check_vma=False,
    )
```

```python
import functools

import jax
import jax.numpy as jnp
from jax import lax
from jax.experimental import pallas as pl
from jax.experimental.pallas import tpu as pltpu
from jax.sharding import PartitionSpec as P

BLK = 64
NB = 256
AXES = ("row", "col")
HIGHEST_PRECISION = lax.Precision.HIGHEST


def locate(index):
    row, col = divmod(index, 16)
    z, y_lo = divmod(row, 2)
    y_hi, rest = divmod(col, 8)
    x, core = divmod(rest, 2)
    return x, y_hi * 2 + y_lo, z, core


def index_of(x, y, z, core):
    y_hi, y_lo = divmod(y, 2)
    return (z % 4 * 2 + y_lo) * 16 + y_hi * 8 + x % 4 * 2 + core


def moves(step, only=lambda x, y, z, core: True):
    return [(i, index_of(*step(*locate(i)))) for i in range(128) if only(*locate(i))]


MOVES = {
    "core": moves(lambda x, y, z, core: (x, y, z, 1 - core)),
    "y_lo": moves(lambda x, y, z, core: (x, y ^ 1, z, core)),
    "y_hi": moves(lambda x, y, z, core: (x, y ^ 2, z, core)),
    "y_both": moves(lambda x, y, z, core: (x, y ^ 3, z, core)),
    "z_far": moves(lambda x, y, z, core: (x, y, z + 2, core)),
    "z_a": moves(lambda x, y, z, core: (x, y, z ^ 1, core)),
    "z_b": moves(lambda x, y, z, core: (x, y, z ^ 3, core)),
    "x_far": moves(lambda x, y, z, core: (x ^ 2, y, z, core)),
    "x_a": moves(lambda x, y, z, core: (x ^ 1, y, z, core)),
    "x_b": moves(lambda x, y, z, core: (x ^ 3, y, z, core)),
}


def deal(e, low):
    def step(x, y, z, core):
        return (z % 2 ^ e) * 2 + y % 2, y // 2 * 2 + core, x, z // 2 ^ low
    return moves(step)


def send(value, move):
    return lax.ppermute(value, AXES, MOVES[move] if isinstance(move, str) else move)


def pick(value, index, axis=0):
    return lax.dynamic_index_in_dim(value, index, axis, keepdims=False)


def total(value, *steps):
    for step in steps:
        value = value + send(value, step)
    return value


def after(value, *earlier):
    return lax.optimization_barrier((value, *earlier))[0]


def mm(a, b, precision=lax.Precision.HIGH):
    return jnp.dot(a, b, precision=precision)


def is_same(shape, scale=1):
    rows = lax.broadcasted_iota(jnp.int32, shape, 0)
    return rows == lax.broadcasted_iota(jnp.int32, shape, 1) // scale


def mask_kernel(places, fock, pattern, out, spread):
    @pl.when(pl.program_id(0) == 0)
    def _():
        same = is_same(spread.shape, BLK).astype(jnp.float32)
        spread[...] = same.astype(jnp.bfloat16)
    row = pattern[pl.ds(places[pl.program_id(0)], 1), :].astype(jnp.float32).astype(jnp.bfloat16)
    row = jnp.broadcast_to(row, (16, row.shape[1]))
    wide = jnp.dot(row, spread[...], preferred_element_type=jnp.float32).astype(jnp.bfloat16)
    out[0] = fock[0] * jnp.broadcast_to(wide[0:1], fock.shape[1:])


def masked_rows(fock, pattern, places):
    blocks, depth = pattern.shape[0], fock.shape[1]
    return pl.pallas_call(
        mask_kernel,
        grid_spec=pltpu.PrefetchScalarGridSpec(
            num_scalar_prefetch=1,
            grid=(blocks,),
            in_specs=[
                pl.BlockSpec((1, BLK, depth), lambda i, places: (places[i], 0, 0)),
                pl.BlockSpec(pattern.shape, lambda i, places: (0, 0)),
            ],
            out_specs=pl.BlockSpec((1, BLK, depth), lambda i, places: (i, 0, 0)),
            scratch_shapes=[pltpu.VMEM((pattern.shape[1], depth), jnp.bfloat16)],
        ),
        out_shape=jax.ShapeDtypeStruct((blocks, BLK, depth), jnp.bfloat16),
        cost_estimate=pl.CostEstimate(flops=10**8, bytes_accessed=4 * fock.size, transcendentals=0),
        compiler_params=pltpu.CompilerParams(vmem_limit_bytes=32 * 2**20),
        name="mask",
    )(places, fock.reshape(blocks, BLK, depth), pattern).reshape(fock.shape)


def eliminate(block, group):
    size = block.shape[0]
    same = is_same((size, size)).astype(jnp.float32)
    work = jnp.concatenate([block, same], axis=1)
    row = lax.broadcasted_iota(jnp.int32, work.shape, 0)
    for start in range(0, size, group):
        columns = [jnp.broadcast_to(work[:, start + i : start + i + 1], work.shape) for i in range(group)]
        for i in range(group):
            at = start + i
            if at == size - 1:
                break
            share = jnp.where(row > at, columns[i] * (1.0 / columns[i][at : at + 1]), 0.0)
            for k in range(i + 1, group):
                columns[k] = columns[k] - share * columns[k][at : at + 1]
            work = work - share * work[at : at + 1]
    pivots = jnp.sum(work[:, :size] * same, axis=1, keepdims=True)
    return work[:, size:] * lax.rsqrt(pivots)


def inverse_kernel(size, gram, out, rest):
    f32_dot = functools.partial(jnp.dot, precision=HIGHEST_PRECISION, preferred_element_type=jnp.float32)
    rest[...] = gram[...]
    out[...] = is_same(out.shape).astype(jnp.float32)
    for lo in range(0, NB, size):
        hi = lo + size
        inverse = eliminate(rest[lo:hi, lo:hi], 16)
        factor = f32_dot(inverse, rest[lo:hi, :])
        done = f32_dot(inverse, out[lo:hi, :])
        out[lo:hi, :] = done
        if hi < NB:
            below = factor.T[hi:, :]
            rest[hi:, :] -= f32_dot(below, factor)
            out[hi:, :] -= f32_dot(below, done)


def inverse_factor(gram):
    return pl.pallas_call(
        functools.partial(inverse_kernel, 64),
        out_shape=jax.ShapeDtypeStruct((NB, NB), jnp.float32),
        scratch_shapes=[pltpu.VMEM((NB, NB), jnp.float32)],
        cost_estimate=pl.CostEstimate(flops=10**10, bytes_accessed=2**19, transcendentals=0),
        compiler_params=pltpu.CompilerParams(vmem_limit_bytes=16 * 2**20),
        name="inverse_factor",
    )(gram)


class Rounds:
    def __init__(self):
        self.last = ()

    def open(self, *values):
        values = lax.optimization_barrier((*values, *self.last))[: len(values)]
        return values[0] if len(values) == 1 else values

    def close(self, *results):
        self.last = results


def body(fock, pattern, coeffs, order):
    row = lax.axis_index("row")
    col = lax.axis_index("col")
    z, y_lo = row // 2, row % 2
    y_hi, x, core = col // 8, col // 2 % 4, col % 2
    z_high, z_low = z // 2, z % 2
    depth = fock.shape[1]
    half = depth // 2
    rounds = Rounds()

    def count(mask, values):
        return jnp.sum(mask.astype(jnp.int32) * values, axis=1)

    slots = jnp.arange(8, dtype=jnp.int32)
    places = jnp.arange(64, dtype=jnp.int32)

    def panel_place(r, s):
        return ((s // 2) ^ x) * 8 + ((r // 2) ^ z) * 2 + r % 2

    def atoms_place(atoms):
        position = count(order[None, :] == atoms[:, None], places[None, :])
        return panel_place(position // 8, position % 8)

    def atoms_of(column_tile):
        return column_tile * 4 + slots[:4]

    dealt_z = 2 * (core ^ (slots // 2 % 2)) + ((x // 2) ^ (slots // 4))
    dealt_places = panel_place(2 * dealt_z + ((slots % 2) ^ (x % 2)), row)
    places_used = [
        jnp.concatenate(
            [
                dealt_places,
                atoms_place(atoms_of(col)),
                *(
                    atoms_place(atoms_of(y_hi * 8 + (2 * (z_low ^ side) + y_lo) * 2 + (core ^ other)))
                    for side in range(2)
                ),
            ]
        )
        for other in range(2)
    ]
    by_row = order.reshape(8, 8)
    trailing = lax.dynamic_slice_in_dim(pick(by_row, 2 * x + core, 1), 2 * z, 2, 0)
    trailing = (trailing >= NB // BLK).astype(jnp.float32)[:, None, None]
    target = pick(by_row, row, 1)
    target = target // 32 * 4 + target % 4
    source = count(target[None, :] == slots[:, None], slots[None, :])
    z_from, y_from = source // 2, source % 2
    dealt = (((x // 2) ^ (z_from % 2)) * 2 + (core ^ (z_from // 2))) * 2 + (y_from ^ (x % 2))

    def product(columns):
        rows = jnp.concatenate([own, peer], axis=0)
        return jnp.dot(rows, columns, preferred_element_type=jnp.float32).reshape(2, 2, 4, BLK, NB)

    def to_other_core(blocks):
        blocks = jnp.stack(blocks)
        return blocks[:, :, 1], send(blocks[:, :, 0], "core")

    def first_over_x(one, two):
        return (
            (one, send(jnp.stack([one[:, 1], one[:, 2]]), "x_a")),
            (two, send(jnp.stack([two[:, 3], two[:, 2]]), "x_b")),
        )

    def second_over_x(first):
        (one, got_one), (two, got_two) = first
        one = jnp.stack([one[:, 0], one[:, 3]]) + got_one
        two = jnp.stack([two[:, 0], two[:, 1]]) + got_two
        return (one[0], send(one[1], "x_b")), (two[0], send(two[1], "x_a"))

    def sums(second):
        return second[0][0] + second[0][1], second[1][0] + second[1][1]

    def landed(parts):
        return parts[0][1], parts[1][1]

    e = jnp.arange(4, dtype=jnp.int32)
    own = masked_rows(fock, pattern, jnp.concatenate([2 * (x ^ e) + 1 - core, 2 * (x ^ e) + core]))
    peer = send(own, "y_lo")
    c0 = coeffs[:, :NB]
    a0, b0 = send(c0, "z_a"), send(c0, "z_b")
    f0, g0 = send(b0[:half], "z_a"), send(a0[half:], "z_b")
    c1 = after(coeffs[:, NB:], a0, b0)
    a1, b1 = send(c1, "z_a"), send(c1, "z_b")
    f1, g1 = send(b1[:half], "z_a"), send(a1[half:], "z_b")
    rounds.close(peer, f0, g0)

    own, peer = rounds.open(own, peer)
    far = jnp.concatenate([f0, g0], axis=0)
    kept, got = to_other_core([product(columns) for columns in (c0, a0, far, b0)])
    kept = kept + got
    first = first_over_x(kept[:, 0], kept[:, 1])
    blocks = [product(after(c1, a1, b1, got))]
    rounds.close(*landed(first), *blocks)
    a1_now, b1_now = rounds.open(a1, b1)
    second = second_over_x(first)
    blocks += [product(a1_now)]
    rounds.close(*landed(second), *blocks)
    both, b1_now = rounds.open(jnp.stack(sums(second), axis=1), b1_now)
    piece = pick(both, z)
    halves = both.reshape(2, 2, *both.shape[1:])
    got = send(jnp.concatenate([pick(halves, z_high ^ y_hi ^ 1), piece[None]]), "y_hi")
    got_lo, got_both = send(piece, "y_lo"), send(piece, "y_both")
    blocks += [product(after(b1_now, f1, g1))]
    rounds.close(got, got_lo, got_both, blocks[2])
    piece, halves, f1 = rounds.open(piece, halves, f1)
    first_part = pick(halves, z_high ^ y_hi) + got[:2]
    piece = jnp.where(y_lo == 0, piece + got[2], got_lo + got_both) * trailing
    ring = [piece, send(piece, "z_a"), send(piece, "z_far"), send(piece, "z_b")]
    blocks.insert(2, product(jnp.concatenate([f1, g1], axis=0)))
    kept, got = to_other_core(blocks)
    rounds.close(got, *ring)
    kept, *ring = rounds.open(kept, *ring)
    ring = jnp.stack(ring)
    ring = [ring, send(ring, "x_a"), send(ring, "x_far"), send(ring, "x_b")]
    kept = (kept + got).reshape(2, 2, 2, 4, BLK, NB)
    got = send(pick(kept, z_high ^ y_hi ^ 1), "y_hi")
    kept = pick(kept, z_high ^ y_hi)
    rounds.close(got, *ring)
    kept, *ring = rounds.open(kept, *ring)
    panel = jnp.stack(ring)
    got_panel = send(panel, "core")
    kept = kept + got
    t1, t2, t3 = send(kept[:, :, 1], "x_a"), send(kept[:, :, 2], "x_far"), send(kept[:, :, 3], "x_b")
    rows_here = panel.reshape(8 * NB, NB)
    rows_there = got_panel.reshape(8 * NB, NB)
    gram = mm(rows_here.T, rows_here) + mm(rows_there.T, rows_there)
    tiles = [
        jnp.take(part.reshape(32, BLK, NB), places_used[other], axis=0)
        for other, part in enumerate((panel, got_panel))
    ]
    panel_rows = jnp.where(core == y_lo, tiles[0][:8], tiles[1][:8]).reshape(2 * NB, NB)
    panel_cols = tiles[0][8:12].reshape(NB, NB)
    tiles = [part[12:].reshape(2, NB, NB) for part in tiles]
    rounds.close(t1, t2, t3, gram, panel_rows, panel_cols, *tiles)
    last_part, gram, *tiles = rounds.open(kept[:, :, 0], gram, *tiles)
    last_part = (last_part + t1) + (t2 + t3)
    both = jnp.stack([first_part, last_part]).reshape(2, 2, 2 * BLK, NB)
    both = [pick(both, core), pick(both, 1 - core)]
    image = 0.0
    for other in range(2):
        for side in range(2):
            image = image + mm(both[other][side], tiles[other][side])
    image = image.reshape(2, BLK, NB)
    image = jnp.where(y_lo == 0, image, image[::-1])
    got_hi, got_lo, got_both = send(image, "y_hi"), send(image, "y_lo"), send(image, "y_both")
    factor_1 = inverse_factor(gram)
    rounds.close(got_hi, got_lo, got_both, factor_1)
    image, factor_1, both[0], both[1] = rounds.open(image, factor_1, *both)
    image = (image + got_hi) + (got_lo + got_both)
    image = jnp.where(y_lo == 0, image, image[::-1]).reshape(2 * BLK, NB)
    both = jnp.stack(both)
    arrived = [
        send(jnp.stack([pick(both[:, side], z_high ^ low ^ core), image]), deal(side, low))
        for side in range(2)
        for low in range(2)
    ]
    once_here, once_there = mm(rows_here, factor_1.T), mm(rows_there, factor_1.T)
    factor_2 = inverse_factor(mm(once_here.T, once_here) + mm(once_there.T, once_there))
    rounds.close(factor_2, *arrived)
    factor_2, *arrived = rounds.open(factor_2, *arrived)
    factor = mm(factor_2, factor_1, HIGHEST_PRECISION).T
    arrived, image = jnp.stack(arrived, axis=1).reshape(2, 2 * NB, NB)
    arrived = arrived - 2.0 * mm(mm(image, factor), mm(panel_cols, factor).T)
    left = mm(panel_rows.T, arrived)
    left = (left + send(left, "z_a")) + (send(left, "z_far") + send(left, "z_b"))
    left = total(left, "y_lo")

    def in_order(value):
        return jnp.take(value.reshape(8, BLK, NB), dealt, axis=0).reshape(2 * NB, NB)

    rows = in_order(mm(mm(panel_rows, factor), factor.T))
    updated = in_order(arrived) - 2.0 * mm(rows, left)
    return updated.reshape(2, NB, NB)


def solution(mesh):
    return jax.shard_map(
        body,
        mesh=mesh,
        in_specs=(P("row", "col"), P("row", "col"), P("col", "row"), P()),
        out_specs=P(None, "row", "col"),
        check_vma=False,
    )
```
